1024 devices in a mesh: row: 16 (over x, y), col: 16 (over z_lo), layer: 4 (over z_hi, core).
Axes of the slice: x: 4, y: 4, z: 32 (z_hi: 2, z_lo: 16; z = z_hi * 16 + z_lo), core: 2. Of those that a mesh axis runs over, the one named last changes fastest.
Arguments:
- slab: bfloat16 [7360, 11776], P(('layer', 'row'), 'col'), may hold values from -6 to 6
- green: bfloat16 [7360, 8832], P(('layer', 'col'), 'row'), may hold values from -0.375 to 0.375
- mask_slab: int32 [320, 512], P(('layer', 'row'), 'col'), may hold values from 0 to 1, as said below
- mask_green: int32 [320, 384], P(('layer', 'col'), 'row'), may hold values from 0 to 1, as said below
Outputs:
- product: bfloat16 [11776, 8832], P('col', ('row', 'layer'))
The draws below stay inside these ranges and needn't reach their ends.
Inputs may be any that keep to these rules, and one draw needn't show every extreme that they name: `mask_slab`: 0 or 1 per atom block. Each device's piece of 5 x 32 atom blocks holds at least one and at most 40 live blocks; some piece holds exactly 40. `mask_green`: 0 or 1 per atom block. Each device's piece of 5 x 24 atom blocks holds at least one and at most 30 live blocks; some piece holds exactly 30.
All inputs are finite; a program needn't handle non-finite values.
Results may differ from the reference program's by a relative error of at most 0.001.
Values may be sent and summed in bfloat16 or wider, within the bound.
A program may use at most 32 MiB of HBM per device.

```python
import jax
import jax.numpy as jnp
from jax import lax

BLK = 23
KB_DEV = 5
MB_DEV = 32
NB_DEV = 24
KORB = 7360
ROWS = 11776
ORBS = 8832
LIVE_SLAB = 40
LIVE_GREEN = 30


def live_pattern(key, piece_rows, piece_cols, block_rows, block_cols, most):
    pieces = piece_rows * piece_cols
    key_count, key_full, key_order = jax.random.split(key, 3)
    least = max(1, most // 4)
    counts = jax.random.randint(key_count, (pieces,), least, most + 1)
    fullest = jax.random.randint(key_full, (), 0, pieces)
    counts = jnp.where(jnp.arange(pieces) == fullest, most, counts)
    order_keys = jax.random.split(key_order, pieces)
    ranks = jax.vmap(lambda single: jax.random.permutation(single, block_rows * block_cols))(order_keys)
    live = (ranks < counts[:, None]).astype(jnp.int32)
    live = live.reshape(piece_rows, piece_cols, block_rows, block_cols)
    live = jnp.transpose(live, (0, 2, 1, 3))
    return live.reshape(piece_rows * block_rows, piece_cols * block_cols)


def draw_mask_slab(key, part):
    key = jax.random.fold_in(key, 11)
    piece_rows = KORB // BLK // KB_DEV
    piece_cols = ROWS // BLK // MB_DEV
    return live_pattern(key, piece_rows, piece_cols, KB_DEV, MB_DEV, LIVE_SLAB)


def draw_mask_green(key, part):
    key = jax.random.fold_in(key, 23)
    piece_rows = KORB // BLK // KB_DEV
    piece_cols = ORBS // BLK // NB_DEV
    return live_pattern(key, piece_rows, piece_cols, KB_DEV, NB_DEV, LIVE_GREEN)


def shard_levels(rng, extent, shards, low, largest):
    factor_of = 1.0
    for position, parts in shards:
        steps = jax.random.uniform(jax.random.fold_in(jax.random.fold_in(rng, 6), position), (parts,), jnp.float32, low / len(shards), largest / len(shards))
        factor_of = factor_of * jnp.repeat(jnp.exp(steps), extent[position] // parts).reshape((-1,) + (1,) * (len(extent) - 1 - position))
    return factor_of


def scatter_about(own_key, extent, spread, most, cuts=(), dtype=jnp.bfloat16):
    values = spread * jax.random.normal(own_key, extent, jnp.float32)
    if cuts:
        values = values * shard_levels(own_key, extent, cuts, -0.22, 0.18)
    return jnp.clip(values, -most, most).astype(dtype)


def setup_inputs(seed: int = 0) -> dict:
    key_list = jax.random.split(jax.random.key(seed), 5)
    slab = scatter_about(key_list[0], (KORB, ROWS), 1.0, 6.0, ((0, 64), (1, 16)))
    green = scatter_about(key_list[1], (KORB, ORBS), (KORB // 32) ** -0.5, 0.375, ((0, 64), (1, 16)))
    mask_slab = draw_mask_slab(jax.random.fold_in(key_list[4], 71), 0)
    mask_green = draw_mask_green(jax.random.fold_in(key_list[4], 71), 0)
    return dict(slab=slab, green=green, mask_slab=mask_slab, mask_green=mask_green)


def expand(mask):
    return jnp.repeat(jnp.repeat(mask, BLK, axis=0), BLK, axis=1).astype(jnp.bfloat16)


def reference(slab, green, mask_slab, mask_green):
    slab_live = slab * expand(mask_slab)
    green_live = green * expand(mask_green)
    total = lax.dot_general(slab_live, green_live, (((0,), (0,)), ((), ())), preferred_element_type=jnp.float32)
    return total.astype(jnp.bfloat16)
```

```python
import functools

import jax
import jax.numpy as jnp
from jax import lax
from jax.experimental import pallas as pl
from jax.experimental.pallas import tpu as pltpu
from jax.sharding import PartitionSpec as P

BLK = 23
KB = 5
PITCH = 24
MB, NB = 32, 24
SLAB_SLOTS, GREEN_SLOTS = 40, 30
SLAB_PER, GREEN_PER = 3, 4
SLAB_TILES, GREEN_TILES = 8, 6
NX, NY, NZ, ZLO = 4, 4, 32, 16
MESH = pl.DeviceIdType.MESH
F32, BF16 = jnp.float32, jnp.bfloat16


def iota(shape, dim):
    return lax.broadcasted_iota(jnp.int32, shape, dim)


def one_hot(where):
    return jnp.where(where, 1.0, 0.0).astype(BF16)


def dot(a, b, dims=((1,), (0,))):
    return lax.dot_general(a, b, (dims, ((), ())), preferred_element_type=F32)


def steps_over(x, edges):
    return sum(jnp.where(x >= e, 1, 0) for e in edges)


def block_codes(mask, blocks, slots, per):
    live = one_hot(mask > 0)
    eye = one_hot(iota((blocks, blocks), 0) == iota((blocks, blocks), 1))
    lower = one_hot(iota((blocks, blocks), 0) >= iota((blocks, blocks), 1))
    live_t = dot(eye, live, ((1,), (1,)))
    live_b = live_t.astype(BF16)
    through = dot(lower, live_b)
    whole = dot(jnp.ones((blocks, blocks), BF16), live_b)
    earlier = dot(whole.astype(BF16), one_hot(iota((KB, KB), 0) < iota((KB, KB), 1)))
    rank = jnp.where(live_t > 0.5, through + earlier - 1.0, -1.0).astype(jnp.int32)
    lane = iota((1, 128), 1)
    slot = lane - slots * steps_over(lane, [slots * q for q in range(1, per)])
    slot = jnp.where(lane < slots * per, slot, -2)
    row = iota((blocks, 128), 0)
    found = jnp.zeros((blocks, 128), F32)
    for kb in range(KB):
        number = (row + (kb * blocks + 1)).astype(F32)
        found = found + jnp.where(rank[:, kb : kb + 1] == slot, number, 0.0)
    return jnp.sum(found, axis=0, keepdims=True).astype(jnp.int32) - 1


def pack(piece, mask, blocks, slots, per, tiles, rows_ref):
    code = block_codes(mask, blocks, slots, per)
    kb = steps_over(code, [blocks * q for q in range(1, KB)])
    block = code - blocks * kb
    lane = iota((1, 128), 1)
    inner = steps_over(lane, [slots * q for q in range(1, per)])
    width = blocks * BLK
    row = iota((width, 128), 0)
    last = iota((PITCH, 128), 0) == BLK
    out = []
    for tile in range(tiles):
        i = per * tile + inner
        source = jnp.where((code >= 0) & (i < BLK), block * BLK + i, -1)
        rows_ref[pl.ds(0, KB * BLK), :] = dot(piece, one_hot(row == source))
        packed = jnp.zeros((PITCH, 128), F32)
        for q in range(KB):
            part = rows_ref[pl.ds(BLK * q, PITCH), :]
            packed = packed + jnp.where(kb == q, part, 0.0)
        out.append(jnp.where(last, code.astype(F32), packed))
    return jnp.concatenate(out, axis=1)


def spread_rows(packet, kb):
    data = iota((PITCH, 256), 0) < BLK
    parts = [jnp.where(data & (kb == q), packet, 0.0) for q in range(KB)]
    parts.append(jnp.zeros((128 - KB * PITCH, 256), F32))
    return jnp.concatenate(parts, axis=0).astype(BF16)


def decode(row, blocks, slots, per):
    code = row.astype(jnp.int32)
    kb = steps_over(code, [blocks * q for q in range(1, KB)])
    lane = iota((1, 256), 1)
    tile = jnp.where(lane >= 128, 1, 0)
    inner = per * tile + steps_over(lane - 128 * tile, [slots * q for q in range(1, per)])
    return code, kb, code - blocks * kb, inner


def unpack_slab(packet):
    code, kb, mb, inner = decode(packet[BLK : BLK + 1, :256], MB, SLAB_SLOTS, SLAB_PER)
    at = jnp.where(code >= 0, inner * MB + mb, -1000)
    row = iota((256, 256), 0)
    low, high = one_hot(row == at), one_hot(row == at + 64)
    groups = [spread_rows(packet[:, 256 * g : 256 * g + 256], kb) for g in range(4)]
    even = dot(jnp.concatenate([groups[0], groups[2]], axis=0), low, ((1,), (1,)))
    odd = dot(jnp.concatenate([groups[1], groups[3]], axis=0), high, ((1,), (1,)))
    out = []
    for h in range(2):
        e, o = even[128 * h : 128 * h + 128], odd[128 * h : 128 * h + 128]
        out += [e[:, :128], e[:, 128:] + o[:, :128], o[:, 128:]]
    return jnp.concatenate(out, axis=1).astype(BF16)


def unpack_green(packet, half):
    code, kb, nb, inner = decode(packet[BLK : BLK + 1, :256], NB, GREEN_SLOTS, GREEN_PER)
    nb = nb - 12 * half
    core = jnp.where(nb >= 6, 1, 0)
    ours = (code >= 0) & (nb >= 0) & (nb < 12)
    at = jnp.where(ours, core * 64 + inner * 6 + nb - 6 * core, -1000)
    place = one_hot(iota((128, 256), 0) == at)
    rows = [spread_rows(packet[:, 256 * g : 256 * g + 256], kb) for g in range(3)]
    out = dot(jnp.concatenate(rows, axis=0), place, ((1,), (1,)))
    return jnp.concatenate([out[128 * g : 128 * g + 128] for g in range(3)], axis=1).astype(BF16)


def put_back(total):
    lane = iota((1, 768), 1)
    source = jnp.where(lane < MB * BLK, (lane % MB) * BLK + lane // MB, -1)
    rows = dot(one_hot(iota((MB * BLK, 768), 0) == source), total, ((1,), (1,)))
    column = iota((1, 6 * BLK), 1)
    nb = steps_over(column, [BLK * q for q in range(1, 6)])
    j = column - BLK * nb
    source = (j // 8) * 64 + (j % 8) * 6 + nb
    return dot(rows.astype(BF16), one_hot(iota((192, 6 * BLK), 0) == source)).astype(BF16)


def kernel(
    slab, green, mask_slab, mask_green, out,
    sbuf, gbuf, relay, slab_all, green_all, acc, other, rows_ref,
    ring_send, ring_recv, hop_send, relay_recv, far_recv, xy_send, xy_recv, pair_sems,
):
    grid_row, zlo, layer = (lax.axis_index(a) for a in ("row", "col", "layer"))
    x, y = grid_row // NY, grid_row % NY
    hi, core = layer // 2, layer % 2
    z = hi * ZLO + zlo
    away = 1 - hi

    def device(xx, yy, zz, cc):
        return (xx * NY + yy, zz % ZLO, (zz // ZLO) * 2 + cc)

    def along(d):
        return device(x, y, (z + d + NZ) % NZ, core)

    beside_x = [device((x + d) % NX, y, z, core) for d in (1, 3, 2)]
    beside_y = [device(x, (y + d) % NY, z, core) for d in (1, 3, 2)]
    sibling = device(x, y, z, 1 - core)
    hops = (8, -8)

    barrier = pltpu.get_barrier_semaphore()
    partners = [along(1), along(-1), along(8), along(-8), *beside_x, *beside_y, sibling]
    for partner in partners:
        pl.semaphore_signal(barrier, inc=1, device_id=partner, device_id_type=MESH)

    def copy(src, dst, send, recv, to):
        return pltpu.make_async_remote_copy(
            src_ref=src, dst_ref=dst, send_sem=send, recv_sem=recv, device_id=to, device_id_type=MESH
        )

    turn = 1 - 2 * core

    def origin(way, step):
        return (z + (2 * way - 1) * turn * step + 2 * NZ) % NZ

    def ring(way, step):
        slot = origin(way, step)
        return copy(
            gbuf.at[slot], gbuf.at[slot], ring_send.at[way, step], ring_recv.at[slot],
            along((1 - 2 * way) * turn),
        )

    def first_hop(side):
        return copy(
            sbuf.at[hi, grid_row, side], relay.at[side], hop_send.at[0, side], relay_recv.at[side], along(hops[side])
        )

    def second_hop(side):
        origin_hi = ((z - hops[side] + NZ) % NZ) // ZLO
        return copy(
            relay.at[side], sbuf.at[origin_hi, grid_row, side], hop_send.at[1, side], far_recv.at[side], along(hops[side])
        )

    def over_x(which, d):
        slot = sbuf.at[which, grid_row]
        return copy(slot, slot, xy_send.at[which, 0, d], xy_recv.at[which, grid_row], beside_x[d])

    def over_y(which, xx, d):
        row = xx * NY + y
        slot = sbuf.at[which, row]
        return copy(slot, slot, xy_send.at[which, 1 + xx, d], xy_recv.at[which, row], beside_y[d])

    def arrived(which, row):
        slot = sbuf.at[which, row]
        copy(slot, slot, xy_send.at[0, 0, 0], xy_recv.at[which, row], sibling).wait_recv()

    def spread_x(which):
        for d in range(3):
            over_x(which, d).start()

    def spread_y(which):
        for d in (1, 2, 3):
            arrived(which, ((x + d) % NX) * NY + y)
        for d in range(3):
            for xx in range(NX):
                over_y(which, xx, d).start()

    def wait_y(which):
        for d in (1, 2, 3):
            for xx in range(NX):
                arrived(which, xx * NY + (y + d) % NY)

    def take_slab(which, row):
        upper = sbuf[which, row, 0].astype(F32)
        lower = sbuf[which, row, 1].astype(F32)
        packet = jnp.concatenate([upper[:PITCH], upper[PITCH:], lower[:PITCH], lower[PITCH:]], axis=1)
        at = pl.multiple_of((which * 16 + row) * 128, 128)
        slab_all[pl.ds(at, 128), :] = unpack_slab(packet)

    def take_green(slot):
        both = gbuf[slot].astype(F32)
        packet = jnp.concatenate([both[:PITCH], both[PITCH:]], axis=1)
        at = pl.multiple_of(slot * 128, 128)
        green_all[pl.ds(at, 128), :] = unpack_green(packet, hi)

    rows_ref[...] = jnp.zeros_like(rows_ref)
    packet = pack(green[...], mask_green[...], NB, GREEN_SLOTS, GREEN_PER, GREEN_TILES, rows_ref)
    gbuf[z] = jnp.concatenate([packet[:, :384], packet[:, 384:]], axis=0).astype(BF16)
    pl.semaphore_wait(barrier, len(partners))
    ring(0, 0).start()
    ring(1, 0).start()

    packet = pack(slab[...], mask_slab[...], MB, SLAB_SLOTS, SLAB_PER, SLAB_TILES, rows_ref)
    for side in range(2):
        quarters = [packet[:, 512 * side + 256 * g : 512 * side + 256 * g + 256] for g in range(2)]
        sbuf[hi, grid_row, side] = jnp.concatenate(quarters, axis=0).astype(BF16)
    first_hop(0).start()
    first_hop(1).start()
    spread_x(hi)
    take_green(z)

    def advance(step, carry):
        copy(gbuf.at[0], gbuf.at[0], ring_send.at[0, 0], ring_recv.at[origin(0, step)], sibling).wait_recv()
        ring(0, step).start()
        copy(gbuf.at[0], gbuf.at[0], ring_send.at[0, 0], ring_recv.at[origin(1, step)], sibling).wait_recv()

        @pl.when(step < 15)
        def _():
            ring(1, step).start()

        @pl.when(step == 2)
        def _():
            spread_y(hi)

        @pl.when(step == 4)
        def _():
            for side in range(2):
                first_hop(side).wait_recv()
                second_hop(side).start()

        @pl.when(step == 5)
        def _():
            wait_y(hi)

        @pl.when(step == 8)
        def _():
            for side in range(2):
                second_hop(side).wait_recv()
            spread_x(away)

        @pl.when(step == 10)
        def _():
            spread_y(away)

        @pl.when(step == 13)
        def _():
            wait_y(away)

        take_green(origin(0, step))
        take_green(origin(1, step))

        @pl.when((step >= 5) & (step < 13))
        def _():
            take_slab(hi, 2 * (step - 5))
            take_slab(hi, 2 * (step - 5) + 1)

        return carry

    lax.fori_loop(1, 16, advance, 0)
    copy(gbuf.at[0], gbuf.at[0], ring_send.at[0, 0], ring_recv.at[origin(0, 16)], sibling).wait_recv()
    take_green(origin(0, 16))

    def rest(row, carry):
        take_slab(away, row)
        return carry

    lax.fori_loop(0, 16, rest, 0)

    acc[...] = jnp.zeros_like(acc)

    def multiply(part, carry):
        at = pl.multiple_of(part * 512, 512)
        left = slab_all[pl.ds(at, 512), :]
        for g in range(3):
            term = dot(green_all[pl.ds(at, 512), 128 * g : 128 * g + 128], left, ((0,), (0,)))
            acc[0, 64 * g : 64 * g + 64, :] += term[:64]
            acc[1, 64 * g : 64 * g + 64, :] += term[64:]
        return carry

    lax.fori_loop(0, 8, multiply, 0)
    swap = copy(acc.at[1 - core], other, pair_sems.at[0], pair_sems.at[1], sibling)
    swap.start()
    swap.wait()
    out[...] = put_back((acc[core] + other[...]).astype(BF16))

    def sent(step, carry):
        ring(0, step).wait_send()

        @pl.when(step < 15)
        def _():
            ring(1, step).wait_send()

        return carry

    lax.fori_loop(0, 16, sent, 0)
    for side in range(2):
        first_hop(side).wait_send()
        second_hop(side).wait_send()
    for which in range(2):
        for d in range(3):
            over_x(which, d).wait_send()
            for xx in range(NX):
                over_y(which, xx, d).wait_send()


def shards(slab, green, mask_slab, mask_green):
    vmem = pl.BlockSpec(memory_space=pltpu.VMEM)
    dma = pltpu.SemaphoreType.DMA
    return pl.pallas_call(
        kernel,
        out_shape=jax.ShapeDtypeStruct((MB * BLK, 6 * BLK), BF16),
        in_specs=[vmem] * 4,
        out_specs=vmem,
        scratch_shapes=[
            pltpu.VMEM((2, 16, 2, 2 * PITCH, 256), BF16),
            pltpu.VMEM((NZ, 2 * PITCH, 384), BF16),
            pltpu.VMEM((2, 2 * PITCH, 256), BF16),
            pltpu.VMEM((32 * 128, 768), BF16),
            pltpu.VMEM((32 * 128, 384), BF16),
            pltpu.VMEM((2, 192, 768), F32),
            pltpu.VMEM((192, 768), F32),
            pltpu.VMEM((120, 128), F32),
            dma((2, 16)),
            dma((NZ,)),
            dma((2, 2)),
            dma((2,)),
            dma((2,)),
            dma((2, 5, 3)),
            dma((2, 16)),
            dma((2,)),
        ],
        compiler_params=pltpu.CompilerParams(
            collective_id=0, has_side_effects=True, vmem_limit_bytes=48 * 1024 * 1024
        ),
        name="block_sparse_product",
    )(slab, green, mask_slab, mask_green)


def solution(mesh):
    in_specs = (
        P(("layer", "row"), "col"),
        P(("layer", "col"), "row"),
        P(("layer", "row"), "col"),
        P(("layer", "col"), "row"),
    )
    out_specs = P("col", ("row", "layer"))
    return jax.shard_map(shards, mesh=mesh, in_specs=in_specs, out_specs=out_specs, check_vma=False)
```

```python
import functools

import jax
import jax.numpy as jnp
from jax import lax
from jax.experimental import pallas as pl
from jax.experimental.pallas import tpu as pltpu
from jax.sharding import PartitionSpec as P

BLK = 23
KB = 5
PITCH = 24
MB, NB = 32, 24
SLAB_SLOTS, GREEN_SLOTS = 40, 30
SLAB_PER, GREEN_PER = 3, 4
SLAB_TILES, GREEN_TILES = 8, 6
NX, NY, NZ, ZLO = 4, 4, 32, 16
MESH = pl.DeviceIdType.MESH
F32, BF16 = jnp.float32, jnp.bfloat16


def iota(shape, dim):
    return lax.broadcasted_iota(jnp.int32, shape, dim)


def one_hot(where):
    return jnp.where(where, 1.0, 0.0).astype(BF16)


def dot(a, b, dims=((1,), (0,))):
    return lax.dot_general(a, b, (dims, ((), ())), preferred_element_type=F32)


def steps_over(x, edges):
    return sum(jnp.where(x >= e, 1, 0) for e in edges)


def block_codes(mask, blocks, slots, per):
    live = one_hot(mask > 0)
    eye = one_hot(iota((blocks, blocks), 0) == iota((blocks, blocks), 1))
    lower = one_hot(iota((blocks, blocks), 0) >= iota((blocks, blocks), 1))
    live_t = dot(eye, live, ((1,), (1,)))
    live_b = live_t.astype(BF16)
    through = dot(lower, live_b)
    whole = dot(jnp.ones((blocks, blocks), BF16), live_b)
    earlier = dot(whole.astype(BF16), one_hot(iota((KB, KB), 0) < iota((KB, KB), 1)))
    rank = jnp.where(live_t > 0.5, through + earlier - 1.0, -1.0).astype(jnp.int32)
    lane = iota((1, 128), 1)
    slot = lane - slots * steps_over(lane, [slots * q for q in range(1, per)])
    slot = jnp.where(lane < slots * per, slot, -2)
    row = iota((blocks, 128), 0)
    found = jnp.zeros((blocks, 128), F32)
    for kb in range(KB):
        number = (row + (kb * blocks + 1)).astype(F32)
        found = found + jnp.where(rank[:, kb : kb + 1] == slot, number, 0.0)
    return jnp.sum(found, axis=0, keepdims=True).astype(jnp.int32) - 1


def pack(piece, mask, blocks, slots, per, tiles, rows_ref, along):
    code = block_codes(mask, blocks, slots, per)
    kb = steps_over(code, [blocks * q for q in range(1, KB)])
    block = code - blocks * kb
    lane = iota((1, 128), 1)
    inner = steps_over(lane, [slots * q for q in range(1, per)])
    width = blocks * BLK
    row = iota((width, 128), 0)
    last = iota((PITCH, 128), 0) == BLK
    out = []
    for tile in range(tiles):
        i = per * tile + inner
        source = jnp.where((code >= 0) & (i < BLK), block * BLK + i, -1)
        rows_ref[pl.ds(0, KB * BLK), :] = dot(piece, one_hot(row == source), ((along,), (0,)))
        packed = jnp.zeros((PITCH, 128), F32)
        for q in range(KB):
            part = rows_ref[pl.ds(BLK * q, PITCH), :]
            packed = packed + jnp.where(kb == q, part, 0.0)
        out.append(jnp.where(last, code.astype(F32), packed))
    return jnp.concatenate(out, axis=1)


def spread_rows(packet, kb):
    data = iota((PITCH, 256), 0) < BLK
    parts = [jnp.where(data & (kb == q), packet, 0.0) for q in range(KB)]
    parts.append(jnp.zeros((128 - KB * PITCH, 256), F32))
    return jnp.concatenate(parts, axis=0).astype(BF16)


def decode(row, blocks, slots, per):
    code = row.astype(jnp.int32)
    kb = steps_over(code, [blocks * q for q in range(1, KB)])
    lane = iota((1, 256), 1)
    tile = jnp.where(lane >= 128, 1, 0)
    inner = per * tile + steps_over(lane - 128 * tile, [slots * q for q in range(1, per)])
    return code, kb, code - blocks * kb, inner


def unpack_slab(packet):
    code, kb, mb, inner = decode(packet[BLK : BLK + 1, :256], MB, SLAB_SLOTS, SLAB_PER)
    at = jnp.where(code >= 0, inner * MB + mb, -1000)
    row = iota((256, 256), 0)
    low, high = one_hot(row == at), one_hot(row == at + 64)
    groups = [spread_rows(packet[:, 256 * g : 256 * g + 256], kb) for g in range(4)]
    even = dot(jnp.concatenate([groups[0], groups[2]], axis=0), low, ((1,), (1,)))
    odd = dot(jnp.concatenate([groups[1], groups[3]], axis=0), high, ((1,), (1,)))
    out = []
    for h in range(2):
        e, o = even[128 * h : 128 * h + 128], odd[128 * h : 128 * h + 128]
        out += [e[:, :128], e[:, 128:] + o[:, :128], o[:, 128:]]
    return jnp.concatenate(out, axis=1).astype(BF16)


def unpack_green(packet, half):
    code, kb, nb, inner = decode(packet[BLK : BLK + 1, :256], NB, GREEN_SLOTS, GREEN_PER)
    nb = nb - 12 * half
    core = jnp.where(nb >= 6, 1, 0)
    ours = (code >= 0) & (nb >= 0) & (nb < 12)
    at = jnp.where(ours, core * 64 + inner * 6 + nb - 6 * core, -1000)
    place = one_hot(iota((128, 256), 0) == at)
    rows = [spread_rows(packet[:, 256 * g : 256 * g + 256], kb) for g in range(3)]
    out = dot(jnp.concatenate(rows, axis=0), place, ((1,), (1,)))
    return jnp.concatenate([out[128 * g : 128 * g + 128] for g in range(3)], axis=1).astype(BF16)


def columns_back():
    lane = iota((1, MB * BLK), 1)
    mb = (lane * 2850) // 65536
    return one_hot(iota((768, MB * BLK), 0) == (lane - BLK * mb) * MB + mb)


def put_back(total, order):
    row = iota((6 * BLK, 192), 0)
    nb = steps_over(row, [BLK * q for q in range(1, 6)])
    j = row - BLK * nb
    source = (j // 8) * 64 + (j % 8) * 6 + nb
    rows = dot(one_hot(iota((6 * BLK, 192), 1) == source), total)
    return dot(rows.astype(BF16), order).astype(BF16)


def kernel(
    slab, green, mask_slab, mask_green, out,
    sbuf, gbuf, relay, slab_all, green_all, acc, other, rows_ref, order,
    chain_send, near_send, ring_recv, hop_send, relay_recv, far_recv, xy_send, xy_recv, pair_sems,
):
    grid_row, zlo, layer = (lax.axis_index(a) for a in ("row", "col", "layer"))
    x, y = grid_row // NY, grid_row % NY
    hi, core = layer // 2, layer % 2
    z = hi * ZLO + zlo
    away = 1 - hi

    def device(xx, yy, zz, cc):
        return (xx * NY + yy, zz % ZLO, (zz // ZLO) * 2 + cc)

    def along(d):
        return device(x, y, (z + d + NZ) % NZ, core)

    beside_x = [device((x + d) % NX, y, z, core) for d in (1, 3, 2)]
    beside_y = [device(x, (y + d) % NY, z, core) for d in (1, 3, 2)]
    sibling = device(x, y, z, 1 - core)
    hops = (8, -8)

    barrier = pltpu.get_barrier_semaphore()
    partners = [*(along(d) for d in (1, -1, 3, -3, 8, -8)), *beside_x, *beside_y, sibling]
    for partner in partners:
        pl.semaphore_signal(barrier, inc=1, device_id=partner, device_id_type=MESH)

    def copy(src, dst, send, recv, to):
        return pltpu.make_async_remote_copy(
            src_ref=src, dst_ref=dst, send_sem=send, recv_sem=recv, device_id=to, device_id_type=MESH
        )

    turn = 1 - 2 * core

    def slot_at(off):
        return (z + turn * off + 2 * NZ) % NZ

    def send_green(off, d, sem):
        slot = slot_at(off)
        return copy(gbuf.at[slot], gbuf.at[slot], sem, ring_recv.at[slot], along(turn * d))

    def chain(way, step):
        sign = 2 * way - 1
        return send_green(sign * 3 * step, -3 * sign, chain_send.at[way, step])

    def near(way, step, d):
        return send_green((2 * way - 1) * 3 * step, d, near_send.at[way, step, (d + 1) // 2])

    def green_arrived(off):
        copy(gbuf.at[0], gbuf.at[0], chain_send.at[0, 0], ring_recv.at[slot_at(off)], sibling).wait_recv()

    def first_hop(side):
        return copy(
            sbuf.at[hi, grid_row, side], relay.at[side], hop_send.at[0, side], relay_recv.at[side], along(hops[side])
        )

    def second_hop(side):
        origin_hi = ((z - hops[side] + NZ) % NZ) // ZLO
        return copy(
            relay.at[side], sbuf.at[origin_hi, grid_row, side], hop_send.at[1, side], far_recv.at[side], along(hops[side])
        )

    def send_slab(which, row, half, sem, to):
        part = sbuf.at[which, row, half]
        return copy(part, part, sem, xy_recv.at[which, row, half], to)

    def first_phase(which, d):
        return [
            send_slab(which, grid_row, 0, xy_send.at[which, 0, 0, d], beside_x[d]),
            send_slab(which, grid_row, 1, xy_send.at[which, 1, 0, d], beside_y[d]),
        ]

    def second_phase(which, q, d):
        return [
            send_slab(which, ((x + q) % NX) * NY + y, 0, xy_send.at[which, 0, 1 + q, d], beside_y[d]),
            send_slab(which, x * NY + (y + q) % NY, 1, xy_send.at[which, 1, 1 + q, d], beside_x[d]),
        ]

    def slab_arrived(which, row, half):
        part = sbuf.at[which, row, half]
        copy(part, part, xy_send.at[0, 0, 0, 0], xy_recv.at[which, row, half], sibling).wait_recv()

    def start_first(which):
        for d in range(3):
            for c in first_phase(which, d):
                c.start()

    def start_second(which):
        for d in (1, 2, 3):
            slab_arrived(which, ((x + d) % NX) * NY + y, 0)
            slab_arrived(which, x * NY + (y + d) % NY, 1)
        for d in range(3):
            for q in range(4):
                for c in second_phase(which, q, d):
                    c.start()

    def wait_second(which):
        for q in range(4):
            for d in (1, 2, 3):
                slab_arrived(which, ((x + q) % NX) * NY + (y + d) % NY, 0)
                slab_arrived(which, ((x + d) % NX) * NY + (y + q) % NY, 1)

    def take_slab(which, row):
        upper = sbuf[which, row, 0].astype(F32)
        lower = sbuf[which, row, 1].astype(F32)
        packet = jnp.concatenate([upper[:PITCH], upper[PITCH:], lower[:PITCH], lower[PITCH:]], axis=1)
        at = pl.multiple_of((which * 16 + row) * 128, 128)
        slab_all[pl.ds(at, 128), :] = unpack_slab(packet)

    def take_green(off):
        slot = slot_at(off)
        both = gbuf[slot].astype(F32)
        packet = jnp.concatenate([both[:PITCH], both[PITCH:]], axis=1)
        at = pl.multiple_of(slot * 128, 128)
        green_all[pl.ds(at, 128), :] = unpack_green(packet, hi)

    def multiply(part):
        at = pl.multiple_of(part * 512, 512)
        left = slab_all[pl.ds(at, 512), :]
        for g in range(3):
            term = dot(green_all[pl.ds(at, 512), 128 * g : 128 * g + 128], left, ((0,), (0,)))
            acc[0, 64 * g : 64 * g + 64, :] += term[:64]
            acc[1, 64 * g : 64 * g + 64, :] += term[64:]

    def loop(start, stop, body):
        lax.fori_loop(start, stop, lambda i, carry: (body(i), carry)[1], 0)

    rows_ref[...] = jnp.zeros_like(rows_ref)
    packet = pack(green[...], mask_green[...], NB, GREEN_SLOTS, GREEN_PER, GREEN_TILES, rows_ref, 0)
    gbuf[z] = jnp.concatenate([packet[:, :384], packet[:, 384:]], axis=0).astype(BF16)
    packet = pack(slab[...], mask_slab[...], MB, SLAB_SLOTS, SLAB_PER, SLAB_TILES, rows_ref, 1)
    for side in range(2):
        quarters = [packet[:, 512 * side + 256 * g : 512 * side + 256 * g + 256] for g in range(2)]
        sbuf[hi, grid_row, side] = jnp.concatenate(quarters, axis=0).astype(BF16)
    pl.semaphore_wait(barrier, len(partners))
    chain(0, 0).start()
    chain(1, 0).start()
    first_hop(0).start()
    first_hop(1).start()
    near(0, 0, 1).start()
    near(0, 0, -1).start()
    start_first(hi)
    order[...] = columns_back()
    acc[...] = jnp.zeros_like(acc)
    take_green(0)

    def advance(step):
        green_arrived(-3 * step)

        @pl.when(step < 5)
        def _():
            chain(0, step).start()

        near(0, step, 1).start()
        near(0, step, -1).start()
        green_arrived(3 * step)

        @pl.when(step < 5)
        def _():
            chain(1, step).start()
            near(1, step, -1).start()

        near(1, step, 1).start()

        @pl.when(step == 1)
        def _():
            start_second(hi)

        @pl.when(step == 2)
        def _():
            for side in range(2):
                first_hop(side).wait_recv()
                second_hop(side).start()

        @pl.when(step == 3)
        def _():
            for side in range(2):
                second_hop(side).wait_recv()
            start_first(away)
            wait_second(hi)

        @pl.when(step == 4)
        def _():
            start_second(away)

        take_green(-3 * step)
        take_green(3 * step)
        before = 3 * (step - 1)
        green_arrived(-before - 1)
        take_green(-before - 1)
        green_arrived(before + 1)
        take_green(before + 1)

        @pl.when(step > 1)
        def _():
            green_arrived(1 - before)
            take_green(1 - before)
            green_arrived(before - 1)
            take_green(before - 1)

        @pl.when(step == 3)
        def _():
            loop(0, 6, lambda row: take_slab(hi, row))

        @pl.when(step == 4)
        def _():
            loop(6, 11, lambda row: take_slab(hi, row))

        @pl.when(step == 5)
        def _():
            loop(11, 16, lambda row: take_slab(hi, row))

    loop(1, 6, advance)
    for off in (-16, -14, 14):
        green_arrived(off)
        take_green(off)
    loop(0, 4, lambda part: multiply(4 * hi + part))
    wait_second(away)
    loop(0, 16, lambda row: take_slab(away, row))
    loop(0, 4, lambda part: multiply(4 * away + part))

    swap = copy(acc.at[1 - core], other, pair_sems.at[0], pair_sems.at[1], sibling)
    swap.start()
    swap.wait()
    out[...] = put_back((acc[core] + other[...]).astype(BF16), order[...])

    for way in range(2):
        for step in range(5):
            chain(way, step).wait_send()
        for step in range(6):
            for d in (-1, 1):
                if (step > 0 or way == 0) and not (way == 1 and step == 5 and d == -1):
                    near(way, step, d).wait_send()
    for side in range(2):
        first_hop(side).wait_send()
        second_hop(side).wait_send()
    for which in range(2):
        for d in range(3):
            for c in first_phase(which, d):
                c.wait_send()
            for q in range(4):
                for c in second_phase(which, q, d):
                    c.wait_send()


def shards(slab, green, mask_slab, mask_green):
    vmem = pl.BlockSpec(memory_space=pltpu.VMEM)
    dma = pltpu.SemaphoreType.DMA
    product = pl.pallas_call(
        kernel,
        out_shape=jax.ShapeDtypeStruct((6 * BLK, MB * BLK), BF16),
        in_specs=[vmem] * 4,
        out_specs=vmem,
        scratch_shapes=[
            pltpu.VMEM((2, 16, 2, 2 * PITCH, 256), BF16),
            pltpu.VMEM((NZ, 2 * PITCH, 384), BF16),
            pltpu.VMEM((2, 2 * PITCH, 256), BF16),
            pltpu.VMEM((32 * 128, 768), BF16),
            pltpu.VMEM((32 * 128, 384), BF16),
            pltpu.VMEM((2, 192, 768), F32),
            pltpu.VMEM((192, 768), F32),
            pltpu.VMEM((120, 128), F32),
            pltpu.VMEM((768, MB * BLK), BF16),
            dma((2, 5)),
            dma((2, 6, 2)),
            dma((NZ,)),
            dma((2, 2)),
            dma((2,)),
            dma((2,)),
            dma((2, 2, 5, 3)),
            dma((2, 16, 2)),
            dma((2,)),
        ],
        compiler_params=pltpu.CompilerParams(
            collective_id=0, has_side_effects=True, vmem_limit_bytes=48 * 1024 * 1024
        ),
        name="block_sparse_product",
    )(slab, green.T, mask_slab, mask_green)
    return product.T


def solution(mesh):
    in_specs = (
        P(("layer", "row"), "col"),
        P(("layer", "col"), "row"),
        P(("layer", "row"), "col"),
        P(("layer", "col"), "row"),
    )
    out_specs = P("col", ("row", "layer"))
    return jax.shard_map(shards, mesh=mesh, in_specs=in_specs, out_specs=out_specs, check_vma=False)
```

```python
import functools

import jax
import jax.numpy as jnp
from jax import lax
from jax.experimental import pallas as pl
from jax.experimental.pallas import tpu as pltpu
from jax.sharding import PartitionSpec as P

BLK = 23
KB = 5
PITCH = 24
MB, NB = 32, 24
SLAB_SLOTS, GREEN_SLOTS = 40, 30
SLAB_PER, GREEN_PER = 3, 4
SLAB_TILES, GREEN_TILES = 8, 6
NX, NY, NZ, ZLO = 4, 4, 32, 16
MESH = pl.DeviceIdType.MESH
F32, BF16 = jnp.float32, jnp.bfloat16


def iota(shape, dim):
    return lax.broadcasted_iota(jnp.int32, shape, dim)


def one_hot(where):
    return jnp.where(where, 1.0, 0.0).astype(BF16)


def dot(a, b, dims=((1,), (0,))):
    return lax.dot_general(a, b, (dims, ((), ())), preferred_element_type=F32)


def steps_over(x, edges):
    return sum(jnp.where(x >= e, 1, 0) for e in edges)


def block_codes(mask, blocks, slots, per):
    live = one_hot(mask > 0)
    eye = one_hot(iota((blocks, blocks), 0) == iota((blocks, blocks), 1))
    lower = one_hot(iota((blocks, blocks), 0) >= iota((blocks, blocks), 1))
    live_t = dot(eye, live, ((1,), (1,)))
    live_b = live_t.astype(BF16)
    through = dot(lower, live_b)
    whole = dot(jnp.ones((blocks, blocks), BF16), live_b)
    earlier = dot(whole.astype(BF16), one_hot(iota((KB, KB), 0) < iota((KB, KB), 1)))
    rank = jnp.where(live_t > 0.5, through + earlier - 1.0, -1.0).astype(jnp.int32)
    lane = iota((1, 128), 1)
    slot = lane - slots * steps_over(lane, [slots * q for q in range(1, per)])
    slot = jnp.where(lane < slots * per, slot, -2)
    row = iota((blocks, 128), 0)
    found = jnp.zeros((blocks, 128), F32)
    for kb in range(KB):
        number = (row + (kb * blocks + 1)).astype(F32)
        found = found + jnp.where(rank[:, kb : kb + 1] == slot, number, 0.0)
    return jnp.sum(found, axis=0, keepdims=True).astype(jnp.int32) - 1


def pack(piece, mask, blocks, slots, per, tiles, rows_ref, along):
    code = block_codes(mask, blocks, slots, per)
    kb = steps_over(code, [blocks * q for q in range(1, KB)])
    block = code - blocks * kb
    lane = iota((1, 128), 1)
    inner = steps_over(lane, [slots * q for q in range(1, per)])
    width = blocks * BLK
    row = iota((width, 128), 0)
    last = iota((PITCH, 128), 0) == BLK
    out = []
    for tile in range(tiles):
        i = per * tile + inner
        source = jnp.where((code >= 0) & (i < BLK), block * BLK + i, -1)
        rows_ref[tile, pl.ds(0, KB * BLK), :] = dot(piece, one_hot(row == source), ((along,), (0,)))
        packed = jnp.zeros((PITCH, 128), F32)
        for q in range(KB):
            part = rows_ref[tile, pl.ds(BLK * q, PITCH), :]
            packed = packed + jnp.where(kb == q, part, 0.0)
        out.append(jnp.where(last, code.astype(F32), packed))
    return jnp.concatenate(out, axis=1)


def spread_rows(packet, kb):
    data = iota((PITCH, 256), 0) < BLK
    parts = [jnp.where(data & (kb == q), packet, 0.0) for q in range(KB)]
    parts.append(jnp.zeros((128 - KB * PITCH, 256), F32))
    return jnp.concatenate(parts, axis=0).astype(BF16)


def decode(row, blocks, slots, per):
    code = row.astype(jnp.int32)
    kb = steps_over(code, [blocks * q for q in range(1, KB)])
    lane = iota((1, 256), 1)
    tile = jnp.where(lane >= 128, 1, 0)
    inner = per * tile + steps_over(lane - 128 * tile, [slots * q for q in range(1, per)])
    return code, kb, code - blocks * kb, inner


def unpack_slab(packet):
    code, kb, mb, inner = decode(packet[BLK : BLK + 1, :256], MB, SLAB_SLOTS, SLAB_PER)
    at = jnp.where(code >= 0, inner * MB + mb, -1000)
    row = iota((256, 256), 0)
    low, high = one_hot(row == at), one_hot(row == at + 64)
    groups = [spread_rows(packet[:, 256 * g : 256 * g + 256], kb) for g in range(4)]
    even = dot(jnp.concatenate([groups[0], groups[2]], axis=0), low, ((1,), (1,)))
    odd = dot(jnp.concatenate([groups[1], groups[3]], axis=0), high, ((1,), (1,)))
    out = []
    for h in range(2):
        e, o = even[128 * h : 128 * h + 128], odd[128 * h : 128 * h + 128]
        out += [e[:, :128], e[:, 128:] + o[:, :128], o[:, 128:]]
    return jnp.concatenate(out, axis=1).astype(BF16)


def unpack_green(packet, half):
    code, kb, nb, inner = decode(packet[BLK : BLK + 1, :256], NB, GREEN_SLOTS, GREEN_PER)
    nb = nb - 12 * half
    core = jnp.where(nb >= 6, 1, 0)
    ours = (code >= 0) & (nb >= 0) & (nb < 12)
    at = jnp.where(ours, core * 64 + inner * 6 + nb - 6 * core, -1000)
    place = one_hot(iota((128, 256), 0) == at)
    rows = [spread_rows(packet[:, 256 * g : 256 * g + 256], kb) for g in range(3)]
    out = dot(jnp.concatenate(rows, axis=0), place, ((1,), (1,)))
    return jnp.concatenate([out[128 * g : 128 * g + 128] for g in range(3)], axis=1).astype(BF16)


def columns_back():
    lane = iota((1, MB * BLK), 1)
    mb = (lane * 2850) // 65536
    return one_hot(iota((768, MB * BLK), 0) == (lane - BLK * mb) * MB + mb)


def put_back(total, order):
    row = iota((6 * BLK, 192), 0)
    nb = steps_over(row, [BLK * q for q in range(1, 6)])
    j = row - BLK * nb
    source = (j // 8) * 64 + (j % 8) * 6 + nb
    rows = dot(one_hot(iota((6 * BLK, 192), 1) == source), total)
    return dot(rows.astype(BF16), order).astype(BF16)


def kernel(
    slab_hbm, green_hbm, mask_slab_hbm, mask_green_hbm, out,
    sbuf, gbuf, relay, slab_all, green_all, acc, other, green_rows, slab_rows, order,
    slab, green, mask_slab, mask_green, in_sems,
    chain_send, near_send, ring_recv, hop_send, relay_recv, far_recv, xy_send, xy_recv, pair_sems,
):
    grid_row, zlo, layer = (lax.axis_index(a) for a in ("row", "col", "layer"))
    x, y = grid_row // NY, grid_row % NY
    hi, core = layer // 2, layer % 2
    z = hi * ZLO + zlo
    away = 1 - hi

    def device(xx, yy, zz, cc):
        return (xx * NY + yy, zz % ZLO, (zz // ZLO) * 2 + cc)

    def along(d):
        return device(x, y, (z + d + NZ) % NZ, core)

    beside_x = [device((x + d) % NX, y, z, core) for d in (1, 3, 2)]
    beside_y = [device(x, (y + d) % NY, z, core) for d in (1, 3, 2)]
    sibling = device(x, y, z, 1 - core)
    hops = (8, -8)

    loads = [
        pltpu.make_async_copy(src, dst, in_sems.at[i])
        for i, (src, dst) in enumerate(
            [(mask_green_hbm, mask_green), (green_hbm, green), (mask_slab_hbm, mask_slab), (slab_hbm, slab)]
        )
    ]
    for load in loads:
        load.start()

    barrier = pltpu.get_barrier_semaphore()
    partners = [*(along(d) for d in (1, -1, 3, -3, 8, -8)), *beside_x, *beside_y, sibling]
    for partner in partners:
        pl.semaphore_signal(barrier, inc=1, device_id=partner, device_id_type=MESH)

    def copy(src, dst, send, recv, to):
        return pltpu.make_async_remote_copy(
            src_ref=src, dst_ref=dst, send_sem=send, recv_sem=recv, device_id=to, device_id_type=MESH
        )

    turn = 1 - 2 * core

    def slot_at(off):
        return (z + turn * off + 2 * NZ) % NZ

    def send_green(off, d, sem):
        slot = slot_at(off)
        return copy(gbuf.at[slot], gbuf.at[slot], sem, ring_recv.at[slot], along(turn * d))

    def chain(way, step):
        sign = 2 * way - 1
        return send_green(sign * 3 * step, -3 * sign, chain_send.at[way, step])

    def near(way, step, d):
        return send_green((2 * way - 1) * 3 * step, d, near_send.at[way, step, (d + 1) // 2])

    def green_arrived(off):
        copy(gbuf.at[0], gbuf.at[0], chain_send.at[0, 0], ring_recv.at[slot_at(off)], sibling).wait_recv()

    def first_hop(side):
        return copy(
            sbuf.at[hi, grid_row, side], relay.at[side], hop_send.at[0, side], relay_recv.at[side], along(hops[side])
        )

    def second_hop(side):
        origin_hi = ((z - hops[side] + NZ) % NZ) // ZLO
        return copy(
            relay.at[side], sbuf.at[origin_hi, grid_row, side], hop_send.at[1, side], far_recv.at[side], along(hops[side])
        )

    def send_slab(which, row, half, sem, to):
        part = sbuf.at[which, row, half]
        return copy(part, part, sem, xy_recv.at[which, row, half], to)

    def first_phase(which, d):
        return [
            send_slab(which, grid_row, 0, xy_send.at[which, 0, 0, d], beside_x[d]),
            send_slab(which, grid_row, 1, xy_send.at[which, 1, 0, d], beside_y[d]),
        ]

    def second_phase(which, q, d):
        return [
            send_slab(which, ((x + q) % NX) * NY + y, 0, xy_send.at[which, 0, 1 + q, d], beside_y[d]),
            send_slab(which, x * NY + (y + q) % NY, 1, xy_send.at[which, 1, 1 + q, d], beside_x[d]),
        ]

    def slab_arrived(which, row, half):
        part = sbuf.at[which, row, half]
        copy(part, part, xy_send.at[0, 0, 0, 0], xy_recv.at[which, row, half], sibling).wait_recv()

    def start_first(which):
        for d in range(3):
            for c in first_phase(which, d):
                c.start()

    def start_second(which):
        for d in (1, 2, 3):
            slab_arrived(which, ((x + d) % NX) * NY + y, 0)
            slab_arrived(which, x * NY + (y + d) % NY, 1)
        for d in range(3):
            for q in range(4):
                for c in second_phase(which, q, d):
                    c.start()

    def wait_second(which):
        for q in range(4):
            for d in (1, 2, 3):
                slab_arrived(which, ((x + q) % NX) * NY + (y + d) % NY, 0)
                slab_arrived(which, ((x + d) % NX) * NY + (y + q) % NY, 1)

    def take_slabs(which, first):
        done = []
        for row in range(4):
            upper = sbuf[which, first + row, 0].astype(F32)
            lower = sbuf[which, first + row, 1].astype(F32)
            done.append(unpack_slab(
                jnp.concatenate([upper[:PITCH], upper[PITCH:], lower[:PITCH], lower[PITCH:]], axis=1)
            ))
        at = pl.multiple_of((which * 16 + first) * 128, 512)
        slab_all[pl.ds(at, 512), :] = jnp.concatenate(done, axis=0)

    def take_greens(offs):
        slots = [slot_at(off) for off in offs]
        done = []
        for slot in slots:
            both = gbuf[slot].astype(F32)
            done.append(unpack_green(jnp.concatenate([both[:PITCH], both[PITCH:]], axis=1), hi))
        for slot, rows in zip(slots, done):
            green_all[pl.ds(pl.multiple_of(slot * 128, 128), 128), :] = rows

    def product(which, tile):
        at = pl.multiple_of(which * 2048, 2048)
        left = slab_all[pl.ds(at, 2048), 256 * tile : 256 * tile + 256]
        return dot(green_all[pl.ds(at, 2048), :], left, ((0,), (0,)))

    def swap(tile):
        part = acc.at[1 - core, :, pl.ds(256 * tile, 256)]
        return copy(part, other.at[:, pl.ds(256 * tile, 256)], pair_sems.at[0, tile], pair_sems.at[1, tile], sibling)

    def loop(start, stop, body):
        lax.fori_loop(start, stop, lambda i, carry: (body(i), carry)[1], 0)

    for rows in (green_rows, slab_rows):
        rows[...] = jnp.zeros_like(rows)
    loads[0].wait()
    loads[1].wait()
    packet = pack(green[...], mask_green[...], NB, GREEN_SLOTS, GREEN_PER, GREEN_TILES, green_rows, 0)
    gbuf[z] = jnp.concatenate([packet[:, :384], packet[:, 384:]], axis=0).astype(BF16)
    loads[2].wait()
    loads[3].wait()
    packet = pack(slab[...], mask_slab[...], MB, SLAB_SLOTS, SLAB_PER, SLAB_TILES, slab_rows, 1)
    for side in range(2):
        quarters = [packet[:, 512 * side + 256 * g : 512 * side + 256 * g + 256] for g in range(2)]
        sbuf[hi, grid_row, side] = jnp.concatenate(quarters, axis=0).astype(BF16)
    pl.semaphore_wait(barrier, len(partners))
    chain(0, 0).start()
    chain(1, 0).start()
    first_hop(0).start()
    first_hop(1).start()
    near(0, 0, 1).start()
    near(0, 0, -1).start()
    start_first(hi)
    order[...] = columns_back()
    take_greens([0])

    def advance(step):
        green_arrived(-3 * step)

        @pl.when(step < 5)
        def _():
            chain(0, step).start()

        near(0, step, 1).start()
        near(0, step, -1).start()
        green_arrived(3 * step)

        @pl.when(step < 5)
        def _():
            chain(1, step).start()
            near(1, step, -1).start()

        near(1, step, 1).start()

        @pl.when(step == 1)
        def _():
            start_second(hi)

        @pl.when(step == 2)
        def _():
            for side in range(2):
                first_hop(side).wait_recv()
                second_hop(side).start()

        @pl.when(step == 3)
        def _():
            for side in range(2):
                second_hop(side).wait_recv()
            start_first(away)
            wait_second(hi)

        @pl.when(step == 4)
        def _():
            start_second(away)

        before = 3 * (step - 1)
        green_arrived(-before - 1)
        green_arrived(before + 1)

        @pl.when(step > 1)
        def _():
            green_arrived(1 - before)
            green_arrived(before - 1)

        take_greens([-3 * step, 3 * step, -before - 1, before + 1, 1 - before, before - 1])

        @pl.when(step == 3)
        def _():
            take_slabs(hi, 0)

        @pl.when(step > 3)
        def _():
            take_slabs(hi, 4 * (step - 3))

    loop(1, 6, advance)
    take_slabs(hi, 12)
    for off in (-16, -14, 14):
        green_arrived(off)
    take_greens([-16, -14, 14])
    for tile in range(3):
        term = product(hi, tile)
        for g in range(3):
            for c in range(2):
                at = 128 * g + 64 * c
                acc[c, 64 * g : 64 * g + 64, 256 * tile : 256 * tile + 256] = term[at : at + 64]
    wait_second(away)
    loop(0, 4, lambda part: take_slabs(away, 4 * part))
    for tile in range(3):
        term = product(away, tile)
        for g in range(3):
            for c in range(2):
                at = 128 * g + 64 * c
                acc[c, 64 * g : 64 * g + 64, 256 * tile : 256 * tile + 256] += term[at : at + 64]
        swap(tile).start()
    for tile in range(3):
        swap(tile).wait()
    out[...] = put_back((acc[core] + other[...]).astype(BF16), order[...])

    for way in range(2):
        for step in range(5):
            chain(way, step).wait_send()
        for step in range(6):
            for d in (-1, 1):
                if (step > 0 or way == 0) and not (way == 1 and step == 5 and d == -1):
                    near(way, step, d).wait_send()
    for side in range(2):
        first_hop(side).wait_send()
        second_hop(side).wait_send()
    for which in range(2):
        for d in range(3):
            for c in first_phase(which, d):
                c.wait_send()
            for q in range(4):
                for c in second_phase(which, q, d):
                    c.wait_send()


def shards(slab, green, mask_slab, mask_green):
    vmem = pl.BlockSpec(memory_space=pltpu.VMEM)
    dma = pltpu.SemaphoreType.DMA
    product = pl.pallas_call(
        kernel,
        out_shape=jax.ShapeDtypeStruct((6 * BLK, MB * BLK), BF16),
        in_specs=[pl.BlockSpec(memory_space=pl.ANY)] * 4,
        out_specs=vmem,
        scratch_shapes=[
            pltpu.VMEM((2, 16, 2, 2 * PITCH, 256), BF16),
            pltpu.VMEM((NZ, 2 * PITCH, 384), BF16),
            pltpu.VMEM((2, 2 * PITCH, 256), BF16),
            pltpu.VMEM((32 * 128, 768), BF16),
            pltpu.VMEM((32 * 128, 384), BF16),
            pltpu.VMEM((2, 192, 768), F32),
            pltpu.VMEM((192, 768), F32),
            pltpu.VMEM((GREEN_TILES, 120, 128), F32),
            pltpu.VMEM((SLAB_TILES, 120, 128), F32),
            pltpu.VMEM((768, MB * BLK), BF16),
            pltpu.VMEM((KB * BLK, MB * BLK), BF16),
            pltpu.VMEM((NB * BLK, KB * BLK), BF16),
            pltpu.VMEM((KB, MB), jnp.int32),
            pltpu.VMEM((KB, NB), jnp.int32),
            dma((4,)),
            dma((2, 5)),
            dma((2, 6, 2)),
            dma((NZ,)),
            dma((2, 2)),
            dma((2,)),
            dma((2,)),
            dma((2, 2, 5, 3)),
            dma((2, 16, 2)),
            dma((2, 3)),
        ],
        compiler_params=pltpu.CompilerParams(
            collective_id=0, has_side_effects=True, vmem_limit_bytes=60 * 1024 * 1024
        ),
        name="block_sparse_product",
    )(slab, green.T, mask_slab, mask_green)
    return product.T


def solution(mesh):
    in_specs = (
        P(("layer", "row"), "col"),
        P(("layer", "col"), "row"),
        P(("layer", "row"), "col"),
        P(("layer", "col"), "row"),
    )
    out_specs = P("col", ("row", "layer"))
    return jax.shard_map(shards, mesh=mesh, in_specs=in_specs, out_specs=out_specs, check_vma=False)
```

```python
import functools

import jax
import jax.numpy as jnp
from jax import lax
from jax.experimental import pallas as pl
from jax.experimental.pallas import tpu as pltpu
from jax.sharding import PartitionSpec as P

BLK = 23
KB = 5
PITCH = 24
MB, NB = 32, 24
SLAB_SLOTS, GREEN_SLOTS = 40, 30
SLAB_PER, GREEN_PER = 3, 4
SLAB_TILES, GREEN_TILES = 8, 6
NX, NY, NZ, ZLO = 4, 4, 32, 16
MESH = pl.DeviceIdType.MESH
F32, BF16 = jnp.float32, jnp.bfloat16


def iota(shape, dim):
    return lax.broadcasted_iota(jnp.int32, shape, dim)


def one_hot(where):
    return jnp.where(where, 1.0, 0.0).astype(BF16)


def dot(a, b, dims=((1,), (0,))):
    return lax.dot_general(a, b, (dims, ((), ())), preferred_element_type=F32)


def steps_over(x, edges):
    return sum(jnp.where(x >= e, 1, 0) for e in edges)


def block_codes(mask, blocks, slots, per):
    live = one_hot(mask > 0)
    eye = one_hot(iota((blocks, blocks), 0) == iota((blocks, blocks), 1))
    lower = one_hot(iota((blocks, blocks), 0) >= iota((blocks, blocks), 1))
    live_t = dot(eye, live, ((1,), (1,)))
    live_b = live_t.astype(BF16)
    through = dot(lower, live_b)
    whole = dot(jnp.ones((blocks, blocks), BF16), live_b)
    earlier = dot(whole.astype(BF16), one_hot(iota((KB, KB), 0) < iota((KB, KB), 1)))
    rank = jnp.where(live_t > 0.5, through + earlier - 1.0, -1.0).astype(jnp.int32)
    lane = iota((1, 128), 1)
    slot = lane - slots * steps_over(lane, [slots * q for q in range(1, per)])
    slot = jnp.where(lane < slots * per, slot, -2)
    row = iota((blocks, 128), 0)
    found = jnp.zeros((blocks, 128), F32)
    for kb in range(KB):
        number = (row + (kb * blocks + 1)).astype(F32)
        found = found + jnp.where(rank[:, kb : kb + 1] == slot, number, 0.0)
    return jnp.sum(found, axis=0, keepdims=True).astype(jnp.int32) - 1


def pack(piece, mask, blocks, slots, per, tiles, rows_ref, along):
    code = block_codes(mask, blocks, slots, per)
    kb = steps_over(code, [blocks * q for q in range(1, KB)])
    block = code - blocks * kb
    lane = iota((1, 128), 1)
    inner = steps_over(lane, [slots * q for q in range(1, per)])
    width = blocks * BLK
    row = iota((width, 128), 0)
    last = iota((PITCH, 128), 0) == BLK
    out = []
    for tile in range(tiles):
        i = per * tile + inner
        source = jnp.where((code >= 0) & (i < BLK), block * BLK + i, -1)
        rows_ref[tile, pl.ds(0, KB * BLK), :] = dot(piece, one_hot(row == source), ((along,), (0,)))
        packed = jnp.zeros((PITCH, 128), F32)
        for q in range(KB):
            part = rows_ref[tile, pl.ds(BLK * q, PITCH), :]
            packed = packed + jnp.where(kb == q, part, 0.0)
        out.append(jnp.where(last, code.astype(F32), packed))
    return jnp.concatenate(out, axis=1)


def spread_rows(packet, kb):
    data = iota((PITCH, 256), 0) < BLK
    parts = [jnp.where(data & (kb == q), packet, 0.0) for q in range(KB)]
    parts.append(jnp.zeros((128 - KB * PITCH, 256), F32))
    return jnp.concatenate(parts, axis=0).astype(BF16)


def decode(row, blocks, slots, per):
    code = row.astype(jnp.int32)
    kb = steps_over(code, [blocks * q for q in range(1, KB)])
    lane = iota((1, 256), 1)
    tile = jnp.where(lane >= 128, 1, 0)
    inner = per * tile + steps_over(lane - 128 * tile, [slots * q for q in range(1, per)])
    return code, kb, code - blocks * kb, inner


def unpack_slab(packet):
    code, kb, mb, inner = decode(packet[BLK : BLK + 1, :256], MB, SLAB_SLOTS, SLAB_PER)
    at = jnp.where(code >= 0, inner * MB + mb, -1000)
    row = iota((256, 256), 0)
    low, high = one_hot(row == at), one_hot(row == at + 64)
    groups = [spread_rows(packet[:, 256 * g : 256 * g + 256], kb) for g in range(4)]
    even = dot(jnp.concatenate([groups[0], groups[2]], axis=0), low, ((1,), (1,)))
    odd = dot(jnp.concatenate([groups[1], groups[3]], axis=0), high, ((1,), (1,)))
    out = []
    for h in range(2):
        e, o = even[128 * h : 128 * h + 128], odd[128 * h : 128 * h + 128]
        out += [e[:, :128], e[:, 128:] + o[:, :128], o[:, 128:]]
    return jnp.concatenate(out, axis=1).astype(BF16)


def unpack_green(packet, half):
    code, kb, nb, inner = decode(packet[BLK : BLK + 1, :256], NB, GREEN_SLOTS, GREEN_PER)
    nb = nb - 12 * half
    core = jnp.where(nb >= 6, 1, 0)
    ours = (code >= 0) & (nb >= 0) & (nb < 12)
    at = jnp.where(ours, core * 64 + inner * 6 + nb - 6 * core, -1000)
    place = one_hot(iota((128, 256), 0) == at)
    rows = [spread_rows(packet[:, 256 * g : 256 * g + 256], kb) for g in range(3)]
    out = dot(jnp.concatenate(rows, axis=0), place, ((1,), (1,)))
    return jnp.concatenate([out[128 * g : 128 * g + 128] for g in range(3)], axis=1).astype(BF16)


def columns_back():
    lane = iota((1, MB * BLK), 1)
    mb = (lane * 2850) // 65536
    return one_hot(iota((768, MB * BLK), 0) == (lane - BLK * mb) * MB + mb)


def put_back(total, order):
    row = iota((6 * BLK, 192), 0)
    nb = steps_over(row, [BLK * q for q in range(1, 6)])
    j = row - BLK * nb
    source = (j // 8) * 64 + (j % 8) * 6 + nb
    rows = dot(one_hot(iota((6 * BLK, 192), 1) == source), total)
    return dot(rows.astype(BF16), order).astype(BF16)


def kernel(
    slab_hbm, green_hbm, mask_slab_hbm, mask_green_hbm, out,
    sbuf, gbuf, relay, slab_all, green_all, acc, other, green_rows, slab_rows, order,
    slab, green, mask_slab, mask_green, in_sems,
    chain_send, near_send, ring_recv, hop_send, relay_recv, far_recv, xy_send, xy_recv, pair_sems,
):
    grid_row, zlo, layer = (lax.axis_index(a) for a in ("row", "col", "layer"))
    x, y = grid_row // NY, grid_row % NY
    hi, core = layer // 2, layer % 2
    z = hi * ZLO + zlo
    away = 1 - hi

    def device(xx, yy, zz, cc):
        return (xx * NY + yy, zz % ZLO, (zz // ZLO) * 2 + cc)

    def along(d):
        return device(x, y, (z + d + NZ) % NZ, core)

    beside_x = [device((x + d) % NX, y, z, core) for d in (1, 3, 2)]
    beside_y = [device(x, (y + d) % NY, z, core) for d in (1, 3, 2)]
    sibling = device(x, y, z, 1 - core)
    hops = (8, -8)

    loads = [
        pltpu.make_async_copy(src, dst, in_sems.at[i])
        for i, (src, dst) in enumerate(
            [(mask_green_hbm, mask_green), (green_hbm, green), (mask_slab_hbm, mask_slab), (slab_hbm, slab)]
        )
    ]
    for load in loads:
        load.start()

    barrier = pltpu.get_barrier_semaphore()
    partners = [*(along(d) for d in (1, -1, 3, -3, 8, -8)), *beside_x, *beside_y, sibling]
    for partner in partners:
        pl.semaphore_signal(barrier, inc=1, device_id=partner, device_id_type=MESH)

    def copy(src, dst, send, recv, to):
        return pltpu.make_async_remote_copy(
            src_ref=src, dst_ref=dst, send_sem=send, recv_sem=recv, device_id=to, device_id_type=MESH
        )

    turn = 1 - 2 * core

    def slot_at(off):
        return (z + turn * off + 2 * NZ) % NZ

    def send_green(off, d, sem):
        slot = slot_at(off)
        return copy(gbuf.at[slot], gbuf.at[slot], sem, ring_recv.at[slot], along(turn * d))

    def chain(way, step):
        sign = 2 * way - 1
        return send_green(sign * 3 * step, -3 * sign, chain_send.at[way, step])

    def near(way, step, d):
        return send_green((2 * way - 1) * 3 * step, d, near_send.at[way, step, (d + 1) // 2])

    def green_arrived(off):
        copy(gbuf.at[0], gbuf.at[0], chain_send.at[0, 0], ring_recv.at[slot_at(off)], sibling).wait_recv()

    def first_hop(side):
        return copy(
            sbuf.at[hi, grid_row, side], relay.at[side], hop_send.at[0, side], relay_recv.at[side], along(hops[side])
        )

    def second_hop(side):
        origin_hi = ((z - hops[side] + NZ) % NZ) // ZLO
        return copy(
            relay.at[side], sbuf.at[origin_hi, grid_row, side], hop_send.at[1, side], far_recv.at[side], along(hops[side])
        )

    def send_slab(which, row, half, sem, to):
        part = sbuf.at[which, row, half]
        return copy(part, part, sem, xy_recv.at[which, row, half], to)

    def first_phase(which, d):
        return [
            send_slab(which, grid_row, 0, xy_send.at[which, 0, 0, d], beside_x[d]),
            send_slab(which, grid_row, 1, xy_send.at[which, 1, 0, d], beside_y[d]),
        ]

    def second_phase(which, q, d):
        return [
            send_slab(which, ((x + q) % NX) * NY + y, 0, xy_send.at[which, 0, 1 + q, d], beside_y[d]),
            send_slab(which, x * NY + (y + q) % NY, 1, xy_send.at[which, 1, 1 + q, d], beside_x[d]),
        ]

    def slab_arrived(which, row, half):
        part = sbuf.at[which, row, half]
        copy(part, part, xy_send.at[0, 0, 0, 0], xy_recv.at[which, row, half], sibling).wait_recv()

    def start_first(which):
        for d in range(3):
            for c in first_phase(which, d):
                c.start()

    def start_second(which):
        for d in (1, 2, 3):
            slab_arrived(which, ((x + d) % NX) * NY + y, 0)
            slab_arrived(which, x * NY + (y + d) % NY, 1)
        for d in range(3):
            for q in range(4):
                for c in second_phase(which, q, d):
                    c.start()

    def row_at(dx, dy):
        return ((x + dx) % NX) * NY + (y + dy) % NY

    def take_second(which, group):
        for dx, dy in group:
            if dy:
                slab_arrived(which, row_at(dx, dy), 0)
            if dx:
                slab_arrived(which, row_at(dx, dy), 1)
        take_slabs(which, [row_at(dx, dy) for dx, dy in group])

    groups = [
        [(0, 0), (0, 3), (3, 0), (3, 3)],
        [(0, 1), (1, 0), (1, 1), (3, 1)],
        [(1, 3), (0, 2), (2, 0), (3, 2)],
        [(2, 3), (1, 2), (2, 1), (2, 2)],
    ]

    def take_slabs(which, rows):
        done = []
        for row in rows:
            upper = sbuf[which, row, 0].astype(F32)
            lower = sbuf[which, row, 1].astype(F32)
            done.append(unpack_slab(
                jnp.concatenate([upper[:PITCH], upper[PITCH:], lower[:PITCH], lower[PITCH:]], axis=1)
            ))
        for row, values in zip(rows, done):
            slab_all[pl.ds(pl.multiple_of((which * 16 + row) * 128, 128), 128), :] = values

    def take_greens(offs):
        slots = [slot_at(off) for off in offs]
        done = []
        for slot in slots:
            both = gbuf[slot].astype(F32)
            done.append(unpack_green(jnp.concatenate([both[:PITCH], both[PITCH:]], axis=1), hi))
        for slot, rows in zip(slots, done):
            green_all[pl.ds(pl.multiple_of(slot * 128, 128), 128), :] = rows

    def product(tile):
        return dot(green_all[...], slab_all[:, 256 * tile : 256 * tile + 256], ((0,), (0,)))

    def swap(tile):
        part = acc.at[1 - core, :, pl.ds(256 * tile, 256)]
        return copy(part, other.at[:, pl.ds(256 * tile, 256)], pair_sems.at[0, tile], pair_sems.at[1, tile], sibling)

    def loop(start, stop, body):
        lax.fori_loop(start, stop, lambda i, carry: (body(i), carry)[1], 0)

    for rows in (green_rows, slab_rows):
        rows[...] = jnp.zeros_like(rows)
    loads[0].wait()
    loads[1].wait()
    packet = pack(green[...], mask_green[...], NB, GREEN_SLOTS, GREEN_PER, GREEN_TILES, green_rows, 0)
    gbuf[z] = jnp.concatenate([packet[:, :384], packet[:, 384:]], axis=0).astype(BF16)
    loads[2].wait()
    loads[3].wait()
    packet = pack(slab[...], mask_slab[...], MB, SLAB_SLOTS, SLAB_PER, SLAB_TILES, slab_rows, 1)
    for side in range(2):
        quarters = [packet[:, 512 * side + 256 * g : 512 * side + 256 * g + 256] for g in range(2)]
        sbuf[hi, grid_row, side] = jnp.concatenate(quarters, axis=0).astype(BF16)
    pl.semaphore_wait(barrier, len(partners))
    chain(0, 0).start()
    chain(1, 0).start()
    first_hop(0).start()
    first_hop(1).start()
    near(0, 0, 1).start()
    near(0, 0, -1).start()
    start_first(hi)
    order[...] = columns_back()
    take_greens([0])

    def advance(step):
        green_arrived(-3 * step)

        @pl.when(step < 5)
        def _():
            chain(0, step).start()

        near(0, step, 1).start()
        near(0, step, -1).start()
        green_arrived(3 * step)

        @pl.when(step < 5)
        def _():
            chain(1, step).start()
            near(1, step, -1).start()

        near(1, step, 1).start()

        @pl.when(step == 1)
        def _():
            start_second(hi)

        @pl.when(step == 3)
        def _():
            for side in range(2):
                second_hop(side).wait_recv()
            start_first(away)

        @pl.when(step == 4)
        def _():
            start_second(away)

        before = 3 * (step - 1)
        green_arrived(-before - 1)
        green_arrived(before + 1)

        @pl.when(step > 1)
        def _():
            green_arrived(1 - before)
            green_arrived(before - 1)

        take_greens([-3 * step, 3 * step, -before - 1, before + 1, 1 - before, before - 1])

        @pl.when(step == 1)
        def _():
            for side in range(2):
                first_hop(side).wait_recv()
                second_hop(side).start()

        @pl.when(step == 3)
        def _():
            take_second(hi, groups[0])

        @pl.when(step == 4)
        def _():
            take_second(hi, groups[1])

        @pl.when(step == 5)
        def _():
            take_second(hi, groups[2])

    loop(1, 6, advance)
    take_second(hi, groups[3])
    for group in groups:
        take_second(away, group)
    for off in (-16, -14, 14):
        green_arrived(off)
    take_greens([-16, -14, 14])
    for tile in range(3):
        term = product(tile)
        for g in range(3):
            for c in range(2):
                at = 128 * g + 64 * c
                acc[c, 64 * g : 64 * g + 64, 256 * tile : 256 * tile + 256] = term[at : at + 64]
        swap(tile).start()
    for tile in range(3):
        swap(tile).wait()
    out[...] = put_back((acc[core] + other[...]).astype(BF16), order[...])

    for way in range(2):
        for step in range(5):
            chain(way, step).wait_send()
        for step in range(6):
            for d in (-1, 1):
                if (step > 0 or way == 0) and not (way == 1 and step == 5 and d == -1):
                    near(way, step, d).wait_send()
    for side in range(2):
        first_hop(side).wait_send()
        second_hop(side).wait_send()
    for which in range(2):
        for d in range(3):
            for c in first_phase(which, d):
                c.wait_send()
            for q in range(4):
                for c in second_phase(which, q, d):
                    c.wait_send()


def shards(slab, green, mask_slab, mask_green):
    vmem = pl.BlockSpec(memory_space=pltpu.VMEM)
    dma = pltpu.SemaphoreType.DMA
    product = pl.pallas_call(
        kernel,
        out_shape=jax.ShapeDtypeStruct((6 * BLK, MB * BLK), BF16),
        in_specs=[pl.BlockSpec(memory_space=pl.ANY)] * 4,
        out_specs=vmem,
        scratch_shapes=[
            pltpu.VMEM((2, 16, 2, 2 * PITCH, 256), BF16),
            pltpu.VMEM((NZ, 2 * PITCH, 384), BF16),
            pltpu.VMEM((2, 2 * PITCH, 256), BF16),
            pltpu.VMEM((32 * 128, 768), BF16),
            pltpu.VMEM((32 * 128, 384), BF16),
            pltpu.VMEM((2, 192, 768), F32),
            pltpu.VMEM((192, 768), F32),
            pltpu.VMEM((GREEN_TILES, 120, 128), F32),
            pltpu.VMEM((SLAB_TILES, 120, 128), F32),
            pltpu.VMEM((768, MB * BLK), BF16),
            pltpu.VMEM((KB * BLK, MB * BLK), BF16),
            pltpu.VMEM((NB * BLK, KB * BLK), BF16),
            pltpu.VMEM((KB, MB), jnp.int32),
            pltpu.VMEM((KB, NB), jnp.int32),
            dma((4,)),
            dma((2, 5)),
            dma((2, 6, 2)),
            dma((NZ,)),
            dma((2, 2)),
            dma((2,)),
            dma((2,)),
            dma((2, 2, 5, 3)),
            dma((2, 16, 2)),
            dma((2, 3)),
        ],
        compiler_params=pltpu.CompilerParams(
            collective_id=0, has_side_effects=True, vmem_limit_bytes=60 * 1024 * 1024
        ),
        name="block_sparse_product",
    )(slab, green.T, mask_slab, mask_green)
    return product.T


def solution(mesh):
    in_specs = (
        P(("layer", "row"), "col"),
        P(("layer", "col"), "row"),
        P(("layer", "row"), "col"),
        P(("layer", "col"), "row"),
    )
    out_specs = P("col", ("row", "layer"))
    return jax.shard_map(shards, mesh=mesh, in_specs=in_specs, out_specs=out_specs, check_vma=False)
```
